32 devices in a mesh: seq: 8 (over z, y), head: 4 (over x, core).
Axes of the slice: x: 2, y: 2, z: 4, core: 2. Of those that a mesh axis runs over, the one named last changes fastest.
Arguments:
- tokens: bfloat16 [12288, 3072], P('seq', 'head'), may hold values from -6 to 6
- w_qkv: bfloat16 [3072, 9216], P(None, 'head'), may hold values from -0.108253175 to 0.108253175
- w_out: bfloat16 [3072, 3072], P('head'), may hold values from -0.109375 to 0.109375
- dest_shard: int32 [6144, 1], replicated, may hold values from 0 to 7; in each aligned block of 768 rows (0 to 767, 768 to 1535, ...) at most 192 rows name the same one
- dest_index: int32 [6144], replicated, may hold values from 0 to 767
- merge_weight: bfloat16 [6144], replicated, may hold values from 0.25 to 2
- shift: float32 [3072], replicated, may hold values from -3 to 3
- scale: float32 [3072], replicated, may hold values from -0.5 to 0.5
- gate: float32 [3072], replicated, may hold values from 0.5 to 1.5
- q_gain: float32 [128], replicated, may hold values from 0.8 to 5
- k_gain: float32 [128], replicated, may hold values from 0.8 to 5
Outputs:
- result: bfloat16 [12288, 3072], P('seq', 'head')
The draws below stay inside these ranges and needn't reach their ends.
Inputs may be any that keep to these rules, and one draw needn't show every extreme that they name: `dest_shard`: in each aligned block of 768 rows (the merged-away tokens of one shard) no shard is named more than 192 times, a bound that some block reaches.
All inputs are finite; a program needn't handle non-finite values.
Results may differ from the reference program's by a relative error of at most 0.015.
Values may be sent and summed in bfloat16 or wider, within the bound.
A program may use at most 320 MiB of HBM per device.

```python
import math
import jax
import jax.numpy as jnp
import numpy as np
from jax import lax

D = 3072
HEADS = 24
HD = 128
HALF = 768
CAP = 192
SOURCES = 6144
TOKENS = 12288
N_SEQ = 8


def draw_w_qkv(key, part):
    key = jax.random.fold_in(key, 11)
    first = jax.random.fold_in(key, 0)
    base = jnp.clip(jax.random.normal(first, (D, HEADS, 3, HD), jnp.float32), -6.0, 6.0)
    return (base * D ** (-0.5)).reshape(D, HEADS * 3 * HD).astype(jnp.bfloat16)


def draw_q_gain(key, part):
    key = jax.random.fold_in(key, 23)
    return jax.random.uniform(key, (HD,), jnp.float32, 0.8, 1.6)


def draw_k_gain(key, part):
    key = jax.random.fold_in(key, 37)
    return jax.random.uniform(key, (HD,), jnp.float32, 0.8, 1.6)


def with_ends(entries, stream_key, low, largest):
    longest = entries.shape.index(max(entries.shape))
    spots = []
    for shift in (0, 1):
        where = [jax.random.randint(jax.random.fold_in(stream_key, axis), (), 0, length) for axis, length in enumerate(entries.shape)]
        where[longest] = (where[longest] + shift) % entries.shape[longest]
        spots.append(tuple(where))
    return entries.at[spots[0]].set(low).at[spots[1]].set(largest)


def block_levels(key, extent, cuts, smallest, largest):
    def one(position, parts):
        draws = jax.random.uniform(jax.random.fold_in(jax.random.fold_in(key, 6), position), (parts,), jnp.float32, smallest / len(cuts), largest / len(cuts))
        return jnp.repeat(jnp.exp(draws), extent[position] // parts).reshape((-1,) + (1,) * (len(extent) - position - 1))

    loudness = one(*cuts[0])
    for cut in cuts[1:]:
        loudness = loudness * one(*cut)
    return loudness


def deal_out(stream_key, own, number, rows, amount, top, limit, lean):
    order = jax.random.permutation(stream_key, amount)
    crowded, usual = portions_of(amount, rows * top, limit, lean, True), portions_of(amount, rows * top, limit, lean, False)
    places = jnp.arange(amount)

    def named(sizes, turn):
        used = int((sizes > 0).sum())
        fixed = max(1, used // 4)
        shifted = fixed + (places - fixed + turn * (used - fixed)) % max(1, amount - fixed)
        return jnp.zeros((amount,), jnp.int32).at[order[jnp.where(places < fixed, places, shifted)]].set(jnp.asarray(sizes, jnp.int32))

    sizes = jnp.where(number % 4 == 0, named(crowded, number // 4), named(usual, number - number // 4 - 1))
    mixed = jax.random.permutation(jax.random.fold_in(own, 3), amount)
    giver, taker = mixed[0:amount // 2 * 2:2], mixed[1:amount // 2 * 2:2]
    margin = jnp.minimum(sizes[giver] - 1, limit - sizes[taker]) // 2
    margin = jnp.where((giver == order[0]) | (taker == order[0]) | (sizes[taker] == 0), 0, jnp.maximum(margin, 0))
    shifted = jax.random.randint(jax.random.fold_in(own, 4), (amount // 2,), 0, 1 << 20) % (margin + 1)
    sizes = sizes.at[giver].add(-shifted).at[taker].add(shifted)
    members = jnp.searchsorted(jnp.cumsum(sizes), jnp.arange(rows * top), side="right").astype(jnp.int32)
    table = members.reshape(top, rows).T
    table = table[jax.random.permutation(jax.random.fold_in(own, 1), rows)]
    turn = jax.random.randint(jax.random.fold_in(own, 2), (rows, 1), 0, top)
    return jnp.take_along_axis(table, (jnp.arange(top)[None, :] + turn) % top, axis=1)


def portions_of(amount, total, limit, lean, full):
    portions = [(1 << 20) // math.isqrt(standing ** lean) + 1 for standing in range(1, amount + 1)]
    largest = limit if full else min(limit, max(-(-total // amount), total * portions[0] // sum(portions)))
    least = 1 if total - largest >= amount - 1 else 0
    holding, surplus = [largest] + [least] * (amount - 1), total - largest - least * (amount - 1)
    while surplus > 0:
        candidates = [i for i in range(1, amount) if holding[i] < largest] or [i for i in range(1, amount) if holding[i] < limit]
        pool, remaining = sum([portions[i] for i in candidates]), surplus
        for i in candidates:
            extra = min(limit - holding[i], max(1, remaining * portions[i] // pool), surplus)
            holding[i] = holding[i] + extra
            surplus = surplus - extra
    return np.array(holding)


def bell_draw(rng, extent, scale, limit, shards=(), kind=jnp.bfloat16):
    level = block_levels(rng, extent, shards, -0.22, 0.18) if shards else 1.0
    entries = jax.random.normal(rng, extent, jnp.float32) * scale * level
    return jnp.minimum(jnp.maximum(entries, -limit), limit).astype(kind)


def setup_inputs(seed: int = 0) -> dict:
    arg_keys = jax.random.split(jax.random.key(seed), 12)
    tokens = bell_draw(arg_keys[0], (TOKENS, D), 1.0, 6.0, ((0, 8), (1, 4)))
    w_qkv = draw_w_qkv(jax.random.fold_in(arg_keys[11], 71), 0)
    w_out = bell_draw(arg_keys[2], (HEADS * HD, D), (HEADS * HD) ** -0.5, 0.109375, ((0, 4),))
    dest_shard_keys = jax.random.split(jax.random.fold_in(arg_keys[3], 1), SOURCES // HALF)
    dest_shard_turns = jax.random.permutation(jax.random.fold_in(arg_keys[3], 3), SOURCES // HALF)
    dest_shard = jax.vmap(lambda own, number: deal_out(jax.random.fold_in(arg_keys[3], 2), own, number, HALF, N_SEQ, 1, CAP, 2))(dest_shard_keys, dest_shard_turns).reshape((SOURCES, 1))
    dest_index = with_ends(jax.random.randint(arg_keys[4], (SOURCES,), 0, HALF), jax.random.fold_in(arg_keys[4], 1), 0, HALF - 1).astype(jnp.int32)
    merge_weight = jnp.clip(jnp.exp(jax.random.uniform(arg_keys[5], (SOURCES,), jnp.float32, math.log(0.25), math.log(2.0))), 0.25, 2.0).astype(jnp.bfloat16)
    shift = bell_draw(arg_keys[6], (D,), 0.5, 3.0, (), jnp.float32)
    scale = jnp.clip(jax.random.uniform(arg_keys[7], (D,), jnp.float32, -0.5, 0.5), -0.5, 0.5)
    gate = jnp.clip(jax.random.uniform(arg_keys[8], (D,), jnp.float32, 0.5, 1.5), 0.5, 1.5)
    q_gain = draw_q_gain(jax.random.fold_in(arg_keys[11], 71), 0)
    k_gain = draw_k_gain(jax.random.fold_in(arg_keys[11], 71), 0)
    return {"tokens": tokens, "w_qkv": w_qkv, "w_out": w_out, "dest_shard": dest_shard, "dest_index": dest_index, "merge_weight": merge_weight, "shift": shift, "scale": scale, "gate": gate, "q_gain": q_gain, "k_gain": k_gain}


eps = 1e-06

def head_norm(values, gain):
    return values * lax.rsqrt(lax.optimization_barrier(jnp.mean(values * values, axis=-1, keepdims=True)) + eps) * gain

def reference(tokens, w_qkv, w_out, dest_shard, dest_index, merge_weight, shift, scale, gate, q_gain, k_gain):
    width = tokens.shape[1]
    blocks = tokens.reshape(N_SEQ, 2 * HALF, width)
    kept = blocks[:, :HALF].reshape(-1, width).astype(jnp.float32)
    moved = blocks[:, HALF:].reshape(-1, width).astype(jnp.float32)
    total_rows = N_SEQ * HALF
    target = dest_shard[:, 0].astype(jnp.int32) * HALF + dest_index.astype(jnp.int32)
    weight = merge_weight.astype(jnp.float32)
    numer = kept + jax.ops.segment_sum(weight[:, None] * moved, target, num_segments=total_rows)
    denom = 1.0 + jax.ops.segment_sum(weight, target, num_segments=total_rows)
    merged = (numer / denom[:, None]).astype(jnp.bfloat16)
    merged_f = merged.astype(jnp.float32)
    mean = lax.optimization_barrier(jnp.mean(merged_f, axis=1, keepdims=True))
    var = lax.optimization_barrier(jnp.mean(merged_f * merged_f, axis=1, keepdims=True)) - mean * mean
    normed = ((merged_f - mean) * lax.rsqrt(var + eps) * (1.0 + scale) + shift).astype(jnp.bfloat16)
    qkv = jnp.dot(normed, w_qkv, preferred_element_type=jnp.float32).reshape(total_rows, HEADS, 3, HD)
    query = head_norm(qkv[:, :, 0], q_gain).astype(jnp.bfloat16)
    keys = head_norm(qkv[:, :, 1], k_gain).astype(jnp.bfloat16)
    values = qkv[:, :, 2].astype(jnp.bfloat16)

    def one_head(operands):
        query_h, key_h, value_h = operands

        def one_block(query_b):
            scores = jnp.dot(query_b, key_h.T, preferred_element_type=jnp.float32) * HD ** (-0.5)
            top = lax.optimization_barrier(jnp.max(scores, axis=1, keepdims=True))
            probs = jnp.exp(scores - top)
            total = lax.optimization_barrier(jnp.sum(probs, axis=1, keepdims=True))
            summed = jnp.dot(probs.astype(jnp.bfloat16), value_h, preferred_element_type=jnp.float32)
            return (summed / total).astype(jnp.bfloat16)
        return lax.map(one_block, query_h.reshape(N_SEQ, HALF, HD))
    heads_out = lax.map(one_head, (query.transpose(1, 0, 2), keys.transpose(1, 0, 2), values.transpose(1, 0, 2)))
    attended = heads_out.reshape(HEADS, total_rows, HD).transpose(1, 0, 2).reshape(total_rows, HEADS * HD)
    proj = jnp.dot(attended, w_out, preferred_element_type=jnp.float32).astype(jnp.bfloat16)
    proj_f = proj.astype(jnp.float32)
    kept_out = kept + gate * proj_f
    moved_out = moved + gate * proj_f[target]
    joined = jnp.concatenate([kept_out.reshape(N_SEQ, HALF, width), moved_out.reshape(N_SEQ, HALF, width)], axis=1)
    return joined.reshape(N_SEQ * 2 * HALF, width).astype(jnp.bfloat16)
```

```python
import functools
import math

import jax
import jax.numpy as jnp
from jax import lax
from jax.experimental import pallas as pl
from jax.experimental.pallas import tpu as pltpu
from jax.sharding import PartitionSpec as P

HD = 128
eps = 1e-06
VMEM_BYTES = 50 * 1024 * 1024


def qkv_kernel(parts, group, x_ref, w_ref, scale_ref, shift_ref, qg_ref, kg_ref, q_ref, k_ref, v_ref, normed_ref):
    half, width = x_ref.shape[1], x_ref.shape[2]
    features = parts * width
    tile = 256

    @pl.when(pl.program_id(0) == 0)
    def _():
        def rows_step(i, carry):
            rows = pl.ds(pl.multiple_of(i * tile, tile), tile)
            total = jnp.zeros((tile, 1), jnp.float32)
            squares = jnp.zeros((tile, 1), jnp.float32)
            for j in range(parts):
                x = x_ref[j, rows, :].astype(jnp.float32)
                total += jnp.sum(x, axis=1, keepdims=True)
                squares += jnp.sum(x * x, axis=1, keepdims=True)
            mean = total / features
            inv = lax.rsqrt(squares / features - mean * mean + eps)
            for j in range(parts):
                cols = slice(j * width, (j + 1) * width)
                x = x_ref[j, rows, :].astype(jnp.float32)
                normed_ref[rows, cols] = (
                    (x - mean) * inv * (1.0 + scale_ref[:, cols]) + shift_ref[:, cols]
                ).astype(jnp.bfloat16)
            return carry

        lax.fori_loop(0, half // tile, rows_step, 0)

    def norm(values, gain):
        return values * lax.rsqrt(jnp.mean(values * values, axis=-1, keepdims=True) + eps) * gain

    def out_step(i, carry):
        rows = pl.ds(pl.multiple_of(i * tile, tile), tile)
        out = jnp.dot(normed_ref[rows, :], w_ref[...], preferred_element_type=jnp.float32)
        for g in range(group):
            base = g * 3 * HD
            cols = slice(g * HD, (g + 1) * HD)
            q_ref[rows, cols] = norm(out[:, base : base + HD], qg_ref[...]).astype(jnp.bfloat16)
            k_ref[rows, cols] = norm(out[:, base + HD : base + 2 * HD], kg_ref[...]).astype(jnp.bfloat16)
            v_ref[rows, cols] = out[:, base + 2 * HD : base + 3 * HD].astype(jnp.bfloat16)
        return carry

    lax.fori_loop(0, half // tile, out_step, 0)


def project_qkv(gathered, w_qkv, scale, shift, q_gain, k_gain):
    parts, half, width = gathered.shape
    depth, cols = w_qkv.shape
    heads = cols // (3 * HD)
    group = 2 if heads % 2 == 0 else 1
    whole = lambda shape: pl.BlockSpec(shape, lambda i: (0,) * len(shape))
    out = jax.ShapeDtypeStruct((half, heads * HD), jnp.bfloat16)
    return pl.pallas_call(
        functools.partial(qkv_kernel, parts, group),
        grid=(heads // group,),
        in_specs=[
            whole((parts, half, width)),
            pl.BlockSpec((depth, group * 3 * HD), lambda i: (0, i)),
            whole((1, depth)),
            whole((1, depth)),
            whole((1, HD)),
            whole((1, HD)),
        ],
        out_specs=[pl.BlockSpec((half, group * HD), lambda i: (0, i))] * 3,
        out_shape=[out] * 3,
        scratch_shapes=[pltpu.VMEM((half, depth), jnp.bfloat16)],
        compiler_params=pltpu.CompilerParams(
            dimension_semantics=("arbitrary",), vmem_limit_bytes=VMEM_BYTES
        ),
        cost_estimate=pl.CostEstimate(
            flops=2 * half * depth * cols, bytes_accessed=2 * depth * cols + 8 * half * depth, transcendentals=0
        ),
    )(gathered, w_qkv, scale[None, :], shift[None, :], q_gain[None, :], k_gain[None, :])


def flash_kernel(blocks, first, last, *refs):
    q_ref = refs[0]
    k_refs = refs[1 : 1 + blocks]
    v_refs = refs[1 + blocks : 1 + 2 * blocks]
    rest = refs[1 + 2 * blocks :]
    factor = HD ** (-0.5) * math.log2(math.e)
    q = q_ref[...]
    scores = [
        lax.dot_general(q, k[...], (((1,), (1,)), ((), ())), preferred_element_type=jnp.float32) for k in k_refs
    ]
    top = functools.reduce(jnp.maximum, [jnp.max(s, axis=1, keepdims=True) for s in scores])
    if not first:
        old = rest[0][:, :1]
        top = jnp.maximum(top, old)
    total = None
    for s, v in zip(scores, v_refs):
        probs = jnp.exp2((s - top) * factor).astype(jnp.bfloat16)
        values = jnp.concatenate([v[...], jnp.ones_like(v)], axis=1)
        term = jnp.dot(probs, values, preferred_element_type=jnp.float32)
        total = term if total is None else total + term
    if not first:
        total = total + rest[1][...] * jnp.exp2((old - top) * factor)
        rest = rest[2:]
    if last:
        rest[0][...] = (total[:, :HD] / total[:, HD:]).astype(jnp.bfloat16)
    else:
        rest[0][...] = jnp.broadcast_to(top, rest[0].shape)
        rest[1][...] = total


def flash(query, keys, values, state, last):
    rows, width = query.shape
    heads = width // HD
    blocks = len(keys)
    count = keys[0].shape[0]
    tile = 256
    first = state is None
    row_spec = pl.BlockSpec((tile, HD), lambda h, i: (i, h))
    acc_spec = pl.BlockSpec((tile, 2 * HD), lambda h, i: (i, h))
    key_spec = pl.BlockSpec((count, HD), lambda h, i: (0, h))
    state_specs = [row_spec, acc_spec]
    state_shapes = [
        jax.ShapeDtypeStruct((rows, width), jnp.float32),
        jax.ShapeDtypeStruct((rows, 2 * width), jnp.float32),
    ]
    state = () if first else tuple(state)
    return pl.pallas_call(
        functools.partial(flash_kernel, blocks, first, last),
        grid=(heads, rows // tile),
        in_specs=[row_spec] + [key_spec] * (2 * blocks) + ([] if first else state_specs),
        out_specs=row_spec if last else state_specs,
        out_shape=jax.ShapeDtypeStruct((rows, width), jnp.bfloat16) if last else state_shapes,
        compiler_params=pltpu.CompilerParams(
            dimension_semantics=("arbitrary", "arbitrary"), vmem_limit_bytes=VMEM_BYTES
        ),
        cost_estimate=pl.CostEstimate(
            flops=8 * rows * count * blocks * width,
            bytes_accessed=4 * count * blocks * width + 16 * rows * width,
            transcendentals=rows * count * blocks * heads,
        ),
    )(query, *keys, *values, *state)


def ring_pairs(shards):
    depth = 4 if shards % 8 == 0 else 1
    across = shards // depth
    order = []
    for y in range(across):
        line = range(depth) if y % 2 == 0 else range(depth - 1, -1, -1)
        order += [z * across + y for z in line]
    right = [(order[i], order[(i + 1) % shards]) for i in range(shards)]
    return right, [(b, a) for a, b in right]


def attend(query, keys, values):
    shards = lax.axis_size("seq")
    right, left = ring_pairs(shards)
    move_right = lambda x: lax.ppermute(x, "seq", right)
    move_left = lambda x: lax.ppermute(x, "seq", left)
    fk, fv, bk, bv = keys, values, keys, values
    state = None
    here_k, here_v = [keys], [values]
    for step in range(1, shards // 2):
        fk, bk, fv, bv = move_right(fk), move_left(bk), move_right(fv), move_left(bv)
        state = flash(query, here_k, here_v, state, False)
        here_k, here_v = [fk, bk], [fv, bv]
    fk, bv = move_right(fk), move_left(bv)
    state = flash(query, here_k, here_v, state, False)
    return flash(query, [fk], [bv], state, True)


def body(
    tokens, w_qkv, w_out, dest_shard, dest_index, merge_weight, shift, scale, gate, q_gain, k_gain
):
    shards = lax.axis_size("seq")
    mine = lax.axis_index("seq")
    feature_part = lax.axis_index("head")
    rows, width = tokens.shape
    half = rows // 2
    capacity = max(2, 2 * half // shards)
    slots_all = shards * capacity
    owner = dest_shard[:, 0].reshape(shards, half)
    index = dest_index.reshape(shards, half)
    weight = merge_weight.astype(jnp.float32).reshape(shards, half)
    my_owner = lax.dynamic_index_in_dim(owner, mine, 0, keepdims=False)
    hot = jnp.concatenate(
        [my_owner[None, :] == jnp.arange(shards)[:, None], owner == mine], axis=0
    ).astype(jnp.bfloat16)
    upper = (jnp.arange(half)[:, None] <= jnp.arange(half)[None, :]).astype(jnp.bfloat16)
    place = jnp.dot(hot, upper, preferred_element_type=jnp.float32).astype(jnp.int32) - 1
    my_rank = jnp.sum(jnp.where(hot[:shards] > 0, place[:shards], 0), axis=0)
    my_slot = my_owner * capacity + my_rank
    rank = place[shards:]
    packer = (jnp.arange(slots_all)[:, None] == my_slot[None, :]).astype(jnp.bfloat16)
    kept = tokens[:half]
    moved = tokens[half:]
    outgoing = jnp.dot(packer, moved, preferred_element_type=jnp.float32).astype(jnp.bfloat16)
    incoming = lax.all_to_all(
        outgoing.reshape(shards, capacity, width), "seq", split_axis=0, concat_axis=0, tiled=True
    )
    incoming = incoming.reshape(slots_all, width)
    chosen = (owner == mine)[:, :, None] & (rank[:, :, None] == jnp.arange(capacity)[None, None, :])
    slot_weight = jnp.sum(jnp.where(chosen, weight[:, :, None], 0.0), axis=1).reshape(slots_all)
    slot_index = jnp.sum(jnp.where(chosen, index[:, :, None], 0), axis=1).reshape(slots_all)
    slot_used = jnp.any(chosen, axis=1).reshape(slots_all)
    target_hot = (jnp.arange(half)[:, None] == slot_index[None, :]) & slot_used[None, :]
    spread = jnp.where(target_hot, slot_weight[None, :], 0.0)
    numer = kept.astype(jnp.float32) + jnp.dot(
        spread.astype(jnp.bfloat16), incoming, preferred_element_type=jnp.float32
    )
    denom = 1.0 + jnp.sum(spread, axis=1, keepdims=True)
    merged = (numer / denom).astype(jnp.bfloat16)
    gathered = lax.all_gather(merged, "head", axis=0, tiled=False)
    query, keys, values = project_qkv(gathered, w_qkv, scale, shift, q_gain, k_gain)
    attended = attend(query, keys, values)
    share = lax.psum_scatter(
        lax.dot_general(
            w_out, attended, (((0,), (1,)), ((), ())), preferred_element_type=jnp.float32
        ).astype(jnp.bfloat16),
        "head",
        scatter_dimension=0,
        tiled=True,
    ).astype(jnp.float32)
    proj = share.T.astype(jnp.bfloat16)
    gate_here = lax.dynamic_slice_in_dim(gate, feature_part * width, width)
    kept_out = kept.astype(jnp.float32) + gate_here * proj.astype(jnp.float32)
    picker = ((jnp.arange(half)[None, :] == slot_index[:, None]) & slot_used[:, None]).astype(
        jnp.bfloat16
    )
    returning = jnp.dot(picker, proj, preferred_element_type=jnp.float32).astype(jnp.bfloat16)
    back = lax.all_to_all(
        returning.reshape(shards, capacity, width), "seq", split_axis=0, concat_axis=0, tiled=True
    ).reshape(slots_all, width)
    moved_proj = lax.dot_general(
        packer, back, (((0,), (0,)), ((), ())), preferred_element_type=jnp.float32
    )
    moved_out = moved.astype(jnp.float32) + gate_here * moved_proj
    return jnp.concatenate([kept_out, moved_out], axis=0).astype(jnp.bfloat16)


def solution(mesh):
    placed = (
        P("seq", "head"),
        P(None, "head"),
        P("head", None),
        P(),
        P(),
        P(),
        P(),
        P(),
        P(),
        P(),
        P(),
    )
    return jax.shard_map(
        body, mesh=mesh, in_specs=placed, out_specs=P("seq", "head"), check_vma=False
    )
```

```python
import functools
import math

import jax
import jax.numpy as jnp
from jax import lax
from jax.experimental import pallas as pl
from jax.experimental.pallas import tpu as pltpu
from jax.sharding import PartitionSpec as P

HD = 128
eps = 1e-06
VMEM_BYTES = 50 * 1024 * 1024


def qkv_kernel(chunks, group, *refs):
    x_refs = refs[:chunks]
    w_ref, scale_ref, shift_ref, qg_ref, kg_ref, q_ref, k_ref, v_ref, normed_ref = refs[chunks:]
    parts, half, width = x_refs[0].shape
    pieces = [
        (x_refs[c], j, slice((j * chunks + c) * width, (j * chunks + c + 1) * width))
        for j in range(parts)
        for c in range(chunks)
    ]
    features = parts * chunks * width
    tile = 256
    out_tile = half // 2

    @pl.when(pl.program_id(0) == 0)
    def _():
        def rows_step(i, carry):
            rows = pl.ds(pl.multiple_of(i * tile, tile), tile)
            total = jnp.zeros((tile, 1), jnp.float32)
            squares = jnp.zeros((tile, 1), jnp.float32)
            for x_ref, j, cols in pieces:
                x = x_ref[j, rows, :].astype(jnp.float32)
                total += jnp.sum(x, axis=1, keepdims=True)
                squares += jnp.sum(x * x, axis=1, keepdims=True)
            mean = total / features
            inv = lax.rsqrt(squares / features - mean * mean + eps)
            for x_ref, j, cols in pieces:
                x = x_ref[j, rows, :].astype(jnp.float32)
                normed_ref[rows, cols] = (
                    (x - mean) * inv * (1.0 + scale_ref[:, cols]) + shift_ref[:, cols]
                ).astype(jnp.bfloat16)
            return carry

        lax.fori_loop(0, half // tile, rows_step, 0)

    def norm(values, gain):
        return values * lax.rsqrt(jnp.mean(values * values, axis=-1, keepdims=True) + eps) * gain

    def out_step(i, carry):
        rows = pl.ds(pl.multiple_of(i * out_tile, out_tile), out_tile)
        out = jnp.dot(normed_ref[rows, :], w_ref[...], preferred_element_type=jnp.float32)
        for g in range(group):
            base = g * 3 * HD
            cols = slice(g * HD, (g + 1) * HD)
            q_ref[rows, cols] = norm(out[:, base : base + HD], qg_ref[...]).astype(jnp.bfloat16)
            k_ref[rows, cols] = norm(out[:, base + HD : base + 2 * HD], kg_ref[...]).astype(jnp.bfloat16)
            v_ref[rows, cols] = out[:, base + 2 * HD : base + 3 * HD].astype(jnp.bfloat16)
        return carry

    lax.fori_loop(0, half // out_tile, out_step, 0)


def project_qkv(gathered, w_qkv, scale, shift, q_gain, k_gain):
    parts, half, width = gathered[0].shape
    depth, cols = w_qkv.shape
    heads = cols // (3 * HD)
    group = 2 if heads % 2 == 0 else 1
    whole = lambda shape: pl.BlockSpec(shape, lambda i: (0,) * len(shape))
    out = jax.ShapeDtypeStruct((half, heads * HD), jnp.bfloat16)
    return pl.pallas_call(
        functools.partial(qkv_kernel, len(gathered), group),
        grid=(heads // group,),
        in_specs=[whole((parts, half, width))] * len(gathered)
        + [
            pl.BlockSpec((depth, group * 3 * HD), lambda i: (0, i)),
            whole((1, depth)),
            whole((1, depth)),
            whole((1, HD)),
            whole((1, HD)),
        ],
        out_specs=[pl.BlockSpec((half, group * HD), lambda i: (0, i))] * 3,
        out_shape=[out] * 3,
        scratch_shapes=[pltpu.VMEM((half, depth), jnp.bfloat16)],
        compiler_params=pltpu.CompilerParams(
            dimension_semantics=("arbitrary",), vmem_limit_bytes=VMEM_BYTES
        ),
        cost_estimate=pl.CostEstimate(
            flops=2 * half * depth * cols, bytes_accessed=2 * depth * cols + 8 * half * depth, transcendentals=0
        ),
    )(*gathered, w_qkv, scale[None, :], shift[None, :], q_gain[None, :], k_gain[None, :])


def flash_kernel(blocks, group, first, last, *refs):
    q_ref = refs[0]
    k_refs = refs[1 : 1 + blocks]
    v_refs = refs[1 + blocks : 1 + 2 * blocks]
    rest = refs[1 + 2 * blocks :]
    factor = HD ** (-0.5) * math.log2(math.e)
    if not first:
        old_top, old_total = rest[:2]
        rest = rest[2:]
    for g in range(group):
        cols = slice(g * HD, (g + 1) * HD)
        wide = slice(2 * g * HD, 2 * (g + 1) * HD)
        q = q_ref[:, cols]
        scores = [
            lax.dot_general(q, k[:, cols], (((1,), (1,)), ((), ())), preferred_element_type=jnp.float32)
            for k in k_refs
        ]
        top = functools.reduce(jnp.maximum, [jnp.max(s, axis=1, keepdims=True) for s in scores])
        if not first:
            old = old_top[:, g * HD : g * HD + 1]
            top = jnp.maximum(top, old)
        total = None
        for s, v in zip(scores, v_refs):
            probs = jnp.exp2((s - top) * factor).astype(jnp.bfloat16)
            value = v[:, cols]
            values = jnp.concatenate([value, jnp.ones_like(value)], axis=1)
            term = jnp.dot(probs, values, preferred_element_type=jnp.float32)
            total = term if total is None else total + term
        if not first:
            total = total + old_total[:, wide] * jnp.exp2((old - top) * factor)
        if last:
            rest[0][:, cols] = (total[:, :HD] / total[:, HD:]).astype(jnp.bfloat16)
        else:
            rest[0][:, cols] = jnp.broadcast_to(top, (top.shape[0], HD))
            rest[1][:, wide] = total


def flash(query, keys, values, state, last):
    rows, width = query.shape
    heads = width // HD
    group = 2 if heads % 2 == 0 else 1
    blocks = len(keys)
    count = keys[0].shape[0]
    tile = 256
    first = state is None
    row_spec = pl.BlockSpec((tile, group * HD), lambda h, i: (i, h))
    acc_spec = pl.BlockSpec((tile, 2 * group * HD), lambda h, i: (i, h))
    key_spec = pl.BlockSpec((count, group * HD), lambda h, i: (0, h))
    state_specs = [row_spec, acc_spec]
    state_shapes = [
        jax.ShapeDtypeStruct((rows, width), jnp.float32),
        jax.ShapeDtypeStruct((rows, 2 * width), jnp.float32),
    ]
    state = () if first else tuple(state)
    return pl.pallas_call(
        functools.partial(flash_kernel, blocks, group, first, last),
        grid=(heads // group, rows // tile),
        in_specs=[row_spec] + [key_spec] * (2 * blocks) + ([] if first else state_specs),
        out_specs=row_spec if last else state_specs,
        out_shape=jax.ShapeDtypeStruct((rows, width), jnp.bfloat16) if last else state_shapes,
        compiler_params=pltpu.CompilerParams(
            dimension_semantics=("arbitrary", "arbitrary"), vmem_limit_bytes=VMEM_BYTES
        ),
        cost_estimate=pl.CostEstimate(
            flops=8 * rows * count * blocks * width,
            bytes_accessed=4 * count * blocks * width + 16 * rows * width,
            transcendentals=rows * count * blocks * heads,
        ),
    )(query, *keys, *values, *state)


def ring_pairs(shards):
    depth = 4 if shards % 8 == 0 else 1
    across = shards // depth
    order = []
    for y in range(across):
        line = range(depth) if y % 2 == 0 else range(depth - 1, -1, -1)
        order += [z * across + y for z in line]
    right = [(order[i], order[(i + 1) % shards]) for i in range(shards)]
    return right, [(b, a) for a, b in right]


def attend(query, keys, values):
    shards = lax.axis_size("seq")
    right, left = ring_pairs(shards)
    move_right = lambda x: lax.ppermute(x, "seq", right)
    move_left = lambda x: lax.ppermute(x, "seq", left)
    fk, fv, bk, bv = keys, values, keys, values
    state = None
    here_k, here_v = [keys], [values]

    def after(x):
        return x if state is None else lax.optimization_barrier((x, state[0]))[0]

    for step in range(1, shards // 2):
        fk, bk, fv, bv = (
            move_right(after(fk)),
            move_left(after(bk)),
            move_right(after(fv)),
            move_left(after(bv)),
        )
        state = flash(query, here_k, here_v, state, False)
        here_k, here_v = [fk, bk], [fv, bv]
    fk, bv = move_right(after(fk)), move_left(after(bv))
    state = flash(query, here_k, here_v, state, False)
    return flash(query, [fk], [bv], state, True)


def body(
    tokens, w_qkv, w_out, dest_shard, dest_index, merge_weight, shift, scale, gate, q_gain, k_gain
):
    shards = lax.axis_size("seq")
    mine = lax.axis_index("seq")
    feature_part = lax.axis_index("head")
    rows, width = tokens.shape
    half = rows // 2
    capacity = max(2, 2 * half // shards)
    slots_all = shards * capacity
    owner = dest_shard[:, 0].reshape(shards, half)
    index = dest_index.reshape(shards, half)
    weight = merge_weight.astype(jnp.float32).reshape(shards, half)
    my_owner = lax.dynamic_index_in_dim(owner, mine, 0, keepdims=False)
    hot = jnp.concatenate(
        [my_owner[None, :] == jnp.arange(shards)[:, None], owner == mine], axis=0
    ).astype(jnp.bfloat16)
    upper = (jnp.arange(half)[:, None] <= jnp.arange(half)[None, :]).astype(jnp.bfloat16)
    place = jnp.dot(hot, upper, preferred_element_type=jnp.float32).astype(jnp.int32) - 1
    my_rank = jnp.sum(jnp.where(hot[:shards] > 0, place[:shards], 0), axis=0)
    my_slot = my_owner * capacity + my_rank
    rank = place[shards:]
    packer = (jnp.arange(slots_all)[:, None] == my_slot[None, :]).astype(jnp.bfloat16)
    parts = lax.axis_size("head")
    chunks = max(1, width // 384)
    piece = width // chunks
    kept = tokens[:half]
    moved = tokens[half:]

    def exchange(x):
        return lax.all_to_all(
            x.reshape(shards, capacity, piece), "seq", split_axis=0, concat_axis=0, tiled=True
        ).reshape(slots_all, piece)

    incoming = []
    for c in range(chunks):
        outgoing = jnp.dot(
            packer, moved[:, c * piece : (c + 1) * piece], preferred_element_type=jnp.float32
        ).astype(jnp.bfloat16)
        incoming.append(exchange(outgoing))
    chosen = (owner == mine)[:, :, None] & (rank[:, :, None] == jnp.arange(capacity)[None, None, :])
    slot_weight = jnp.sum(jnp.where(chosen, weight[:, :, None], 0.0), axis=1).reshape(slots_all)
    slot_index = jnp.sum(jnp.where(chosen, index[:, :, None], 0), axis=1).reshape(slots_all)
    slot_used = jnp.any(chosen, axis=1).reshape(slots_all)
    target_hot = (jnp.arange(half)[:, None] == slot_index[None, :]) & slot_used[None, :]
    spread = jnp.where(target_hot, slot_weight[None, :], 0.0)
    spread_b = spread.astype(jnp.bfloat16)
    denom = 1.0 + jnp.sum(spread, axis=1, keepdims=True)
    gathered = []
    for c in range(chunks):
        numer = kept[:, c * piece : (c + 1) * piece].astype(jnp.float32) + jnp.dot(
            spread_b, incoming[c], preferred_element_type=jnp.float32
        )
        merged = (numer / denom).astype(jnp.bfloat16)
        gathered.append(lax.all_gather(merged, "head", axis=0, tiled=False))
    query, keys, values = project_qkv(gathered, w_qkv, scale, shift, q_gain, k_gain)
    attended = attend(query, keys, values)
    gate_here = lax.dynamic_slice_in_dim(gate, feature_part * width, width)
    picker = ((jnp.arange(half)[None, :] == slot_index[:, None]) & slot_used[:, None]).astype(
        jnp.bfloat16
    )
    w_parts = w_out.reshape(w_out.shape[0], parts, chunks, piece)
    shares = [
        lax.psum_scatter(
            lax.dot_general(
                w_parts[:, :, c].reshape(w_out.shape[0], parts * piece),
                attended,
                (((0,), (1,)), ((), ())),
                preferred_element_type=jnp.float32,
            ).astype(jnp.bfloat16),
            "head",
            scatter_dimension=0,
            tiled=True,
        )
        for c in range(chunks)
    ]
    kept_out, moved_out = [], []
    for c in range(chunks):
        cols = slice(c * piece, (c + 1) * piece)
        proj = shares[c].T
        returning = jnp.dot(picker, proj, preferred_element_type=jnp.float32).astype(jnp.bfloat16)
        back = exchange(returning)
        kept_out.append(kept[:, cols].astype(jnp.float32) + gate_here[cols] * proj.astype(jnp.float32))
        moved_proj = lax.dot_general(
            packer, back, (((0,), (0,)), ((), ())), preferred_element_type=jnp.float32
        )
        moved_out.append(moved[:, cols].astype(jnp.float32) + gate_here[cols] * moved_proj)
    return jnp.concatenate(
        [
            jnp.concatenate(kept_out, axis=1).astype(jnp.bfloat16),
            jnp.concatenate(moved_out, axis=1).astype(jnp.bfloat16),
        ],
        axis=0,
    )


def solution(mesh):
    placed = (
        P("seq", "head"),
        P(None, "head"),
        P("head", None),
        P(),
        P(),
        P(),
        P(),
        P(),
        P(),
        P(),
        P(),
    )
    return jax.shard_map(
        body, mesh=mesh, in_specs=placed, out_specs=P("seq", "head"), check_vma=False
    )
```

```python
import functools
import math

import jax
import jax.numpy as jnp
from jax import lax
from jax.experimental import pallas as pl
from jax.experimental.pallas import tpu as pltpu
from jax.sharding import PartitionSpec as P

HD = 128
eps = 1e-06
VMEM_BYTES = 50 * 1024 * 1024


def qkv_kernel(chunks, group, *refs):
    x_refs = refs[:chunks]
    w_ref, scale_ref, shift_ref, qg_ref, kg_ref, q_ref, k_ref, v_ref, normed_ref = refs[chunks:]
    parts, half, width = x_refs[0].shape
    pieces = [
        (x_refs[c], j, slice((j * chunks + c) * width, (j * chunks + c + 1) * width))
        for j in range(parts)
        for c in range(chunks)
    ]
    features = parts * chunks * width
    tile = 256
    out_tile = half // 2

    @pl.when(pl.program_id(0) == 0)
    def _():
        def rows_step(i, carry):
            rows = pl.ds(pl.multiple_of(i * tile, tile), tile)
            total = jnp.zeros((tile, 1), jnp.float32)
            squares = jnp.zeros((tile, 1), jnp.float32)
            for x_ref, j, cols in pieces:
                x = x_ref[j, rows, :].astype(jnp.float32)
                total += jnp.sum(x, axis=1, keepdims=True)
                squares += jnp.sum(x * x, axis=1, keepdims=True)
            mean = total / features
            inv = lax.rsqrt(squares / features - mean * mean + eps)
            for x_ref, j, cols in pieces:
                x = x_ref[j, rows, :].astype(jnp.float32)
                normed_ref[rows, cols] = (
                    (x - mean) * inv * (1.0 + scale_ref[:, cols]) + shift_ref[:, cols]
                ).astype(jnp.bfloat16)
            return carry

        lax.fori_loop(0, half // tile, rows_step, 0)

    def norm(values, gain):
        return values * lax.rsqrt(jnp.mean(values * values, axis=-1, keepdims=True) + eps) * gain

    def out_step(i, carry):
        rows = pl.ds(pl.multiple_of(i * out_tile, out_tile), out_tile)
        out = jnp.dot(normed_ref[rows, :], w_ref[...], preferred_element_type=jnp.float32)
        for g in range(group):
            base = g * 3 * HD
            cols = slice(g * HD, (g + 1) * HD)
            q_ref[rows, cols] = norm(out[:, base : base + HD], qg_ref[...]).astype(jnp.bfloat16)
            k_ref[rows, cols] = norm(out[:, base + HD : base + 2 * HD], kg_ref[...]).astype(jnp.bfloat16)
            v_ref[rows, cols] = out[:, base + 2 * HD : base + 3 * HD].astype(jnp.bfloat16)
        return carry

    lax.fori_loop(0, half // out_tile, out_step, 0)


def project_qkv(gathered, w_qkv, scale, shift, q_gain, k_gain):
    parts, half, width = gathered[0].shape
    depth, cols = w_qkv.shape
    heads = cols // (3 * HD)
    group = 2 if heads % 2 == 0 else 1
    whole = lambda shape: pl.BlockSpec(shape, lambda i: (0,) * len(shape))
    out = jax.ShapeDtypeStruct((half, heads * HD), jnp.bfloat16)
    return pl.pallas_call(
        functools.partial(qkv_kernel, len(gathered), group),
        grid=(heads // group,),
        in_specs=[whole((parts, half, width))] * len(gathered)
        + [
            pl.BlockSpec((depth, group * 3 * HD), lambda i: (0, i)),
            whole((1, depth)),
            whole((1, depth)),
            whole((1, HD)),
            whole((1, HD)),
        ],
        out_specs=[pl.BlockSpec((half, group * HD), lambda i: (0, i))] * 3,
        out_shape=[out] * 3,
        scratch_shapes=[pltpu.VMEM((half, depth), jnp.bfloat16)],
        compiler_params=pltpu.CompilerParams(
            dimension_semantics=("arbitrary",), vmem_limit_bytes=VMEM_BYTES
        ),
        cost_estimate=pl.CostEstimate(
            flops=2 * half * depth * cols, bytes_accessed=2 * depth * cols + 8 * half * depth, transcendentals=0
        ),
    )(*gathered, w_qkv, scale[None, :], shift[None, :], q_gain[None, :], k_gain[None, :])


def flash_kernel(blocks, group, first, last, *refs):
    q_ref = refs[0]
    k_refs = refs[1 : 1 + blocks]
    v_refs = refs[1 + blocks : 1 + 2 * blocks]
    rest = refs[1 + 2 * blocks :]
    factor = HD ** (-0.5) * math.log2(math.e)
    if not first:
        old_top, old_total = rest[:2]
        rest = rest[2:]
    for g in range(group):
        cols = slice(g * HD, (g + 1) * HD)
        wide = slice(2 * g * HD, 2 * (g + 1) * HD)
        q = q_ref[:, cols]
        scores = [
            lax.dot_general(q, k[:, cols], (((1,), (1,)), ((), ())), preferred_element_type=jnp.float32)
            for k in k_refs
        ]
        top = functools.reduce(jnp.maximum, [jnp.max(s, axis=1, keepdims=True) for s in scores])
        if not first:
            old = old_top[:, g * HD : g * HD + 1]
            top = jnp.maximum(top, old)
        total = None
        for s, v in zip(scores, v_refs):
            probs = jnp.exp2((s - top) * factor).astype(jnp.bfloat16)
            value = v[:, cols]
            values = jnp.concatenate([value, jnp.ones_like(value)], axis=1)
            term = jnp.dot(probs, values, preferred_element_type=jnp.float32)
            total = term if total is None else total + term
        if not first:
            total = total + old_total[:, wide] * jnp.exp2((old - top) * factor)
        if last:
            rest[0][:, cols] = (total[:, :HD] / total[:, HD:]).astype(jnp.bfloat16)
        else:
            rest[0][:, cols] = jnp.broadcast_to(top, (top.shape[0], HD))
            rest[1][:, wide] = total


def flash(query, keys, values, state, last):
    rows, width = query.shape
    heads = width // HD
    group = 2 if heads % 2 == 0 else 1
    blocks = len(keys)
    count = keys[0].shape[0]
    tile = 256
    first = state is None
    row_spec = pl.BlockSpec((tile, group * HD), lambda h, i: (i, h))
    acc_spec = pl.BlockSpec((tile, 2 * group * HD), lambda h, i: (i, h))
    key_spec = pl.BlockSpec((count, group * HD), lambda h, i: (0, h))
    state_specs = [row_spec, acc_spec]
    state_shapes = [
        jax.ShapeDtypeStruct((rows, width), jnp.float32),
        jax.ShapeDtypeStruct((rows, 2 * width), jnp.float32),
    ]
    state = () if first else tuple(state)
    return pl.pallas_call(
        functools.partial(flash_kernel, blocks, group, first, last),
        grid=(heads // group, rows // tile),
        in_specs=[row_spec] + [key_spec] * (2 * blocks) + ([] if first else state_specs),
        out_specs=row_spec if last else state_specs,
        out_shape=jax.ShapeDtypeStruct((rows, width), jnp.bfloat16) if last else state_shapes,
        compiler_params=pltpu.CompilerParams(
            dimension_semantics=("arbitrary", "arbitrary"), vmem_limit_bytes=VMEM_BYTES
        ),
        cost_estimate=pl.CostEstimate(
            flops=8 * rows * count * blocks * width,
            bytes_accessed=4 * count * blocks * width + 16 * rows * width,
            transcendentals=rows * count * blocks * heads,
        ),
    )(query, *keys, *values, *state)


def ring_pairs(shards):
    depth = 4 if shards % 8 == 0 else 1
    across = shards // depth
    order = []
    for y in range(across):
        line = range(depth) if y % 2 == 0 else range(depth - 1, -1, -1)
        order += [z * across + y for z in line]
    right = [(order[i], order[(i + 1) % shards]) for i in range(shards)]
    return right, [(b, a) for a, b in right]


def attend(query, keys, values):
    shards = lax.axis_size("seq")
    right, left = ring_pairs(shards)
    move_right = lambda x: lax.ppermute(x, "seq", right)
    move_left = lambda x: lax.ppermute(x, "seq", left)
    fk, fv, bk, bv = keys, values, keys, values
    state = None
    here_k, here_v = [keys], [values]

    def after(x):
        return x if state is None else lax.optimization_barrier((x, state[0]))[0]

    for step in range(1, shards // 2):
        fk, bk, fv, bv = (
            move_right(after(fk)),
            move_left(after(bk)),
            move_right(after(fv)),
            move_left(after(bv)),
        )
        state = flash(query, here_k, here_v, state, False)
        here_k, here_v = [fk, bk], [fv, bv]
    fk, bv = move_right(after(fk)), move_left(after(bv))
    state = flash(query, here_k, here_v, state, False)
    return flash(query, [fk], [bv], state, True)


def body(
    tokens, w_qkv, w_out, dest_shard, dest_index, merge_weight, shift, scale, gate, q_gain, k_gain
):
    shards = lax.axis_size("seq")
    mine = lax.axis_index("seq")
    feature_part = lax.axis_index("head")
    rows, width = tokens.shape
    half = rows // 2
    capacity = max(2, 2 * half // shards)
    slots_all = shards * capacity
    owner = dest_shard[:, 0].reshape(shards, half)
    index = dest_index.reshape(shards, half)
    weight = merge_weight.astype(jnp.float32).reshape(shards, half)
    my_owner = lax.dynamic_index_in_dim(owner, mine, 0, keepdims=False)
    hot = jnp.concatenate(
        [my_owner[None, :] == jnp.arange(shards)[:, None], owner == mine], axis=0
    ).astype(jnp.bfloat16)
    upper = (jnp.arange(half)[:, None] <= jnp.arange(half)[None, :]).astype(jnp.bfloat16)
    place = jnp.dot(hot, upper, preferred_element_type=jnp.float32).astype(jnp.int32) - 1
    my_rank = jnp.sum(jnp.where(hot[:shards] > 0, place[:shards], 0), axis=0)
    my_slot = my_owner * capacity + my_rank
    rank = place[shards:]
    packer = (jnp.arange(slots_all)[:, None] == my_slot[None, :]).astype(jnp.bfloat16)
    parts = lax.axis_size("head")
    chunks = max(1, width // 384)
    piece = width // chunks
    kept = tokens[:half]
    moved = tokens[half:]

    def exchange(x):
        return lax.all_to_all(
            x.reshape(shards, capacity, piece), "seq", split_axis=0, concat_axis=0, tiled=True
        ).reshape(slots_all, piece)

    incoming = []
    for c in range(chunks):
        outgoing = jnp.dot(
            packer, moved[:, c * piece : (c + 1) * piece], preferred_element_type=jnp.float32
        ).astype(jnp.bfloat16)
        incoming.append(exchange(outgoing))
    chosen = (owner == mine)[:, :, None] & (rank[:, :, None] == jnp.arange(capacity)[None, None, :])
    slot_weight = jnp.sum(jnp.where(chosen, weight[:, :, None], 0.0), axis=1).reshape(slots_all)
    slot_index = jnp.sum(jnp.where(chosen, index[:, :, None], 0), axis=1).reshape(slots_all)
    slot_used = jnp.any(chosen, axis=1).reshape(slots_all)
    target_hot = (jnp.arange(half)[:, None] == slot_index[None, :]) & slot_used[None, :]
    spread = jnp.where(target_hot, slot_weight[None, :], 0.0)
    spread_b = spread.astype(jnp.bfloat16)
    denom = 1.0 + jnp.sum(spread, axis=1, keepdims=True)
    gathered = []
    for c in range(chunks):
        numer = kept[:, c * piece : (c + 1) * piece].astype(jnp.float32) + jnp.dot(
            spread_b, incoming[c], preferred_element_type=jnp.float32
        )
        merged = (numer / denom).astype(jnp.bfloat16)
        gathered.append(lax.all_gather(merged, "head", axis=0, tiled=False))
    query, keys, values = project_qkv(gathered, w_qkv, scale, shift, q_gain, k_gain)
    attended = attend(query, keys, values)
    gate_here = lax.dynamic_slice_in_dim(gate, feature_part * width, width)
    picker = ((jnp.arange(half)[None, :] == slot_index[:, None]) & slot_used[:, None]).astype(
        jnp.bfloat16
    )
    shares = [
        lax.psum_scatter(
            jnp.concatenate(
                [
                    jnp.dot(
                        attended,
                        w_out[:, p * width + c * piece : p * width + (c + 1) * piece],
                        preferred_element_type=jnp.float32,
                    ).astype(jnp.bfloat16)
                    for p in range(parts)
                ],
                axis=0,
            ),
            "head",
            scatter_dimension=0,
            tiled=True,
        )
        for c in range(chunks)
    ]
    kept_out, moved_out = [], []
    for c in range(chunks):
        cols = slice(c * piece, (c + 1) * piece)
        proj = shares[c]
        returning = jnp.dot(picker, proj, preferred_element_type=jnp.float32).astype(jnp.bfloat16)
        back = exchange(returning)
        kept_out.append(kept[:, cols].astype(jnp.float32) + gate_here[cols] * proj.astype(jnp.float32))
        moved_proj = lax.dot_general(
            packer, back, (((0,), (0,)), ((), ())), preferred_element_type=jnp.float32
        )
        moved_out.append(moved[:, cols].astype(jnp.float32) + gate_here[cols] * moved_proj)
    return jnp.concatenate(
        [
            jnp.concatenate(kept_out, axis=1).astype(jnp.bfloat16),
            jnp.concatenate(moved_out, axis=1).astype(jnp.bfloat16),
        ],
        axis=0,
    )


def solution(mesh):
    placed = (
        P("seq", "head"),
        P(None, "head"),
        P("head", None),
        P(),
        P(),
        P(),
        P(),
        P(),
        P(),
        P(),
        P(),
    )
    return jax.shard_map(
        body, mesh=mesh, in_specs=placed, out_specs=P("seq", "head"), check_vma=False
    )
```
